512 devices in a mesh: row: 8 (over x, y_hi), col: 64 (over y_lo, z, core).
Axes of the slice: x: 4, y: 8 (y_hi: 2, y_lo: 4; y = y_hi * 4 + y_lo), z: 8, core: 2. Of those that a mesh axis runs over, the one named last changes fastest.
Arguments:
- row_emb: float32 [300, 4096], P(None, ('row', 'col')), may hold values from -1.5 to 1.5
- row_acc: float32 [300, 4096], P(None, ('row', 'col')), may hold values from 0.05 to 0.5
- col_emb: float32 [300, 65536], P(None, ('col', 'row')), may hold values from -1.5 to 1.5
- col_acc: float32 [300, 65536], P(None, ('col', 'row')), may hold values from 0.05 to 0.5
- counts: int32 [4096, 65536], P('row', 'col'), may hold values from 0 to 1000, as said below
- row_marg: int32 [4096], P('row'), may hold values from 100 to 9999
- col_marg: int32 [65536], P('col'), may hold values from 100 to 9999
Outputs:
- row_emb_out: float32 [300, 4096], P(None, ('row', 'col'))
- row_acc_out: float32 [300, 4096], P(None, ('row', 'col'))
- col_emb_out: float32 [300, 65536], P(None, ('col', 'row'))
- col_acc_out: float32 [300, 65536], P(None, ('col', 'row'))
The draws below stay inside these ranges and needn't reach their ends.
Inputs may be any that keep to these rules, and one draw needn't show every extreme that they name: Roughly half of the counts are zero.
All inputs are finite; a program needn't handle non-finite values.
Results may differ from the reference program's by a relative error of at most 0.0076.
Values may be sent and summed in bfloat16 or wider, within the bound.
No kernel may reach another device: no remote copies, remote signals or barrier semaphores. Data moves between devices by JAX's collectives and lax.ppermute only.
A program may use at most 64 MiB of HBM per device.

```python
import math
import jax
import jax.numpy as jnp
from jax import lax

D = 300
NROWS = 4096
NCOLS = 65536
N_ROW = 8


def draw_counts(key, part):
    key = jax.random.fold_in(key, 5)
    first, second = jax.random.split(key)
    keep = jax.random.randint(first, (NROWS, NCOLS), 0, 2)
    values = jax.random.randint(second, (NROWS, NCOLS), 1, 1001)
    result = (keep * values).astype(jnp.int32)
    return result.at[0, 0].set(1000)


def place_ends(entries, rng, low, top_value):
    shape = entries.shape
    spot = [jax.random.randint(jax.random.fold_in(rng, axis), (), 0, shape[axis]) for axis in range(len(shape))]
    entries = entries.at[tuple(spot)].set(low)
    longest = shape.index(max(shape))
    spot[longest] = (spot[longest] + 1) % shape[longest]
    return entries.at[tuple(spot)].set(top_value)


def block_scale(rng, shape, cuts, least, largest):
    def one(position, parts):
        heights = jax.random.uniform(jax.random.fold_in(jax.random.fold_in(rng, 6), position), (parts,), jnp.float32, least / len(cuts), largest / len(cuts))
        return jnp.repeat(jnp.exp(heights), shape[position] // parts).reshape((-1,) + (1,) * (len(shape) - position - 1))

    gain = one(*cuts[0])
    for cut in cuts[1:]:
        gain = gain * one(*cut)
    return gain


def noise(rng, dims, scale, limit, shards=(), dtype=jnp.bfloat16):
    gain = block_scale(rng, dims, shards, -0.22, 0.18) if shards else 1.0
    entries = jax.random.normal(rng, dims, jnp.float32) * scale * gain
    return jnp.minimum(jnp.maximum(entries, -limit), limit).astype(dtype)


def setup_inputs(seed: int = 0) -> dict:
    splits = jax.random.split(jax.random.key(seed), 8)
    return {
        "row_emb": noise(splits[0], (D, NROWS), 0.25, 1.5, ((1, 512),), jnp.float32),
        "row_acc": jnp.clip(jnp.exp(math.log(0.5) - 2.3025851 * jax.random.uniform(splits[1], (D, NROWS), jnp.float32) ** block_scale(splits[1], (D, NROWS), ((1, 512),), -0.2, 0.2)), 0.05, 0.5),
        "col_emb": noise(splits[2], (D, NCOLS), 0.25, 1.5, ((1, 512),), jnp.float32),
        "col_acc": jnp.clip(jnp.exp(math.log(0.5) - 2.3025851 * jax.random.uniform(splits[3], (D, NCOLS), jnp.float32) ** block_scale(splits[3], (D, NCOLS), ((1, 512),), -0.2, 0.2)), 0.05, 0.5),
        "counts": draw_counts(jax.random.fold_in(splits[7], 71), 0),
        "row_marg": place_ends(jax.random.randint(splits[5], (NROWS,), 100, 10000), jax.random.fold_in(splits[5], 1), 100, 9999).astype(jnp.int32),
        "col_marg": place_ends(jax.random.randint(splits[6], (NCOLS,), 100, 10000), jax.random.fold_in(splits[6], 1), 100, 9999).astype(jnp.int32),
    }


def pair_slope(score, counts, row_marg, col_marg):
    values = counts.astype(jnp.float32)
    pmi = jnp.log(jnp.maximum(values, 1.0)) + 12.0 - jnp.log(row_marg.astype(jnp.float32))[:, None] - jnp.log(col_marg.astype(jnp.float32))[None, :]
    diff = score - pmi
    weight = 0.1 + 0.25 * jnp.sqrt(values)
    return jnp.where(counts > 0, weight * diff, jax.nn.sigmoid(diff))

def half_copy(values):
    rounded = lax.optimization_barrier(values.astype(jnp.bfloat16))
    return rounded.astype(jnp.float32)

def adagrad(emb, acc, grad):
    acc = acc + grad * grad
    return (emb - 0.1 * grad / jnp.sqrt(acc), acc)

def reference(row_emb, row_acc, col_emb, col_acc, counts, row_marg, col_marg):
    width = row_emb.shape[0]
    blocks = N_ROW
    block_rows = row_emb.shape[1] // blocks
    num_rows = row_emb.shape[1]
    num_cols = col_emb.shape[1]
    count_blocks = counts.reshape(blocks, block_rows, num_cols)
    marg_blocks = row_marg.reshape(blocks, block_rows)
    for step in range(2):
        row_half = half_copy(row_emb)
        col_half = half_copy(col_emb)
        row_parts = jnp.transpose(row_half.reshape(width, blocks, block_rows), (1, 0, 2))

        def one_block(carry, inputs):
            part, block_counts, block_marg = inputs
            score = jnp.dot(part.T, col_half, precision=lax.Precision.HIGHEST, preferred_element_type=jnp.float32)
            slope = half_copy(pair_slope(score, block_counts, block_marg, col_marg))
            grad_rows = jnp.dot(col_half, slope.T, precision=lax.Precision.HIGHEST, preferred_element_type=jnp.float32)
            carry = carry + jnp.dot(part, slope, precision=lax.Precision.HIGHEST, preferred_element_type=jnp.float32)
            return (carry, grad_rows)
        start = jnp.zeros((width, num_cols), jnp.float32)
        col_grad, row_parts_grad = lax.scan(one_block, start, (row_parts, count_blocks, marg_blocks))
        row_grad = jnp.transpose(row_parts_grad, (1, 0, 2)).reshape(width, num_rows)
        row_grad = row_grad / jnp.sqrt(jnp.float32(num_cols))
        col_grad = col_grad / jnp.sqrt(jnp.float32(num_rows))
        row_emb, row_acc = adagrad(row_emb, row_acc, row_grad)
        col_emb, col_acc = adagrad(col_emb, col_acc, col_grad)
    return (row_emb, row_acc, col_emb, col_acc)
```

```python
import jax
import jax.numpy as jnp
from jax import lax
from jax.sharding import PartitionSpec as P


def pair_slope(score, counts, log_row, log_col):
    values = counts.astype(jnp.float32)
    pmi = jnp.log(jnp.maximum(values, 1.0)) + 12.0 - log_row[:, None] - log_col[None, :]
    diff = score - pmi
    weight = 0.1 + 0.25 * jnp.sqrt(values)
    return jnp.where(counts > 0, weight * diff, jax.nn.sigmoid(diff))


def gather(shard, axis):
    size = lax.axis_size(axis)
    return lax.all_to_all(jnp.broadcast_to(shard[None], (size,) + shard.shape), axis, 0, 0)


def scatter_sum(parts, axis):
    return jnp.sum(lax.all_to_all(parts, axis, 0, 0).astype(jnp.float32), axis=0)


def adagrad(emb, acc, grad):
    acc = acc + grad * grad
    return (emb - 0.1 * grad / jnp.sqrt(acc), acc)


def on_device(row_emb, row_acc, col_emb, col_acc, counts, row_marg, col_marg):
    n_row, n_col = lax.axis_size("row"), lax.axis_size("col")
    width = row_emb.shape[0]
    rows, cols = counts.shape
    row_scale = 1.0 / jnp.sqrt(jnp.float32(cols * n_col))
    col_scale = 1.0 / jnp.sqrt(jnp.float32(rows * n_row))
    log_row = jnp.log(row_marg.astype(jnp.float32))
    log_col = jnp.log(col_marg.astype(jnp.float32))
    row_emb, row_acc = row_emb.T, row_acc.T
    for step in range(2):
        row_half = gather(row_emb.astype(jnp.bfloat16), "col").reshape(rows, width)
        col_half = gather(col_emb.astype(jnp.bfloat16), "row").transpose(1, 0, 2).reshape(width, cols)
        score = jnp.dot(row_half, col_half, preferred_element_type=jnp.float32)
        slope = pair_slope(score, counts, log_row, log_col).astype(jnp.bfloat16)
        grad_rows = lax.dot_general(
            slope, col_half, (((1,), (1,)), ((), ())), preferred_element_type=jnp.float32
        ).astype(jnp.bfloat16)
        grad_cols = lax.dot_general(
            row_half, slope, (((0,), (0,)), ((), ())), preferred_element_type=jnp.float32
        ).astype(jnp.bfloat16)
        row_grad = scatter_sum(grad_rows.reshape(n_col, rows // n_col, width), "col") * row_scale
        grad_cols = grad_cols.reshape(width, n_row, cols // n_row).transpose(1, 0, 2)
        col_grad = scatter_sum(grad_cols, "row") * col_scale
        row_emb, row_acc = adagrad(row_emb, row_acc, row_grad)
        col_emb, col_acc = adagrad(col_emb, col_acc, col_grad)
    return (row_emb.T, row_acc.T, col_emb, col_acc)


def solution(mesh):
    by_row, by_col = P(None, ("row", "col")), P(None, ("col", "row"))
    return jax.shard_map(
        on_device,
        mesh=mesh,
        in_specs=(by_row, by_row, by_col, by_col, P("row", "col"), P("row"), P("col")),
        out_specs=(by_row, by_row, by_col, by_col),
        check_vma=False,
    )
```

```python
import jax
import jax.numpy as jnp
from jax import lax
from jax.experimental import pallas as pl
from jax.experimental.pallas import tpu as pltpu
from jax.sharding import PartitionSpec as P

ROW_TILE = 128
VMEM_LIMIT = 24 * 1024 * 1024


def tile_kernel(place, rows_in, piece0, piece1, piece2, piece3, counts_in, row_term_in, col_term_in,
                rows_out, grad0, grad1, grad2, grad3,
                rows, rows_t, cols, counts, row_term, col_term, slope,
                grad_rows, grad_own, grad_away, in_sem, out_sem):
    n_rows = rows.shape[0]
    wide = piece0.shape[1]
    pieces = (piece0, piece1, piece2, piece3)
    outs = (grad0, grad1, grad2, grad3)

    def start(source, target, sem):
        copy = pltpu.make_async_copy(source, target, sem)
        copy.start()
        return copy

    def there(d):
        return pl.ds(pl.multiple_of(lax.rem(place[0] + d, 4) * wide, wide), wide)

    here = [pl.ds(d * wide, wide) for d in range(4)]
    rows_copy = start(rows_in, rows, in_sem.at[0])
    cols_copy, counts_copy = [], []
    for d in range(4):
        cols_copy.append(start(pieces[d], cols.at[:, here[d]], in_sem.at[1 + d]))
        counts_copy.append(
            start(counts_in.at[:, there(d)], counts.at[:, here[d]], in_sem.at[5 + d])
        )
        if d == 0:
            row_copy = start(row_term_in, row_term, in_sem.at[9])
            col_copy = start(col_term_in, col_term, in_sem.at[10])
    rows_copy.wait()
    rows_t[...] = rows[...].T
    done = []
    for d in range(4):
        cols_copy[d].wait()
        counts_copy[d].wait()
        if d == 0:
            row_copy.wait()
            col_copy.wait()
        col_part = col_term[:, there(d)]
        for first in range(0, n_rows, ROW_TILE):
            at = pl.ds(first, ROW_TILE)
            score = jnp.dot(rows[at, :], cols[:, here[d]], preferred_element_type=jnp.float32)
            count = counts[at, here[d]]
            value = jnp.maximum(count.astype(jnp.float32), 1.0)
            diff = score - (jnp.log(value) + (row_term[at, :] - col_part))
            weight = 0.1 + 0.25 * (value * lax.rsqrt(value))
            zero = 0.5 * jnp.tanh(0.5 * diff) + 0.5
            slope[at, here[d]] = jnp.where(count > 0, weight * diff, zero).astype(jnp.bfloat16)
        grad = jnp.dot(rows_t[...], slope[:, here[d]], preferred_element_type=jnp.float32)
        if d == 0:
            grad_own[...] = grad
            done.append(start(grad_own, outs[0], out_sem.at[0]))
        else:
            grad_away[d - 1] = grad.astype(jnp.bfloat16)
            done.append(start(grad_away.at[d - 1], outs[d], out_sem.at[d]))
    grad_rows[...] = lax.dot_general(
        slope[...], cols[...], (((1,), (1,)), ((), ())), preferred_element_type=jnp.float32
    ).astype(jnp.bfloat16)
    done.append(start(grad_rows, rows_out, out_sem.at[4]))
    for copy in done:
        copy.wait()


def tile_grads(place, rows, pieces, counts, row_term, col_term):
    n_rows, width = rows.shape
    wide = pieces[0].shape[1]
    hbm = pl.BlockSpec(memory_space=pltpu.HBM)
    out = jax.ShapeDtypeStruct((width, wide), jnp.bfloat16)
    return pl.pallas_call(
        tile_kernel,
        in_specs=[pl.BlockSpec(memory_space=pltpu.SMEM)] + [hbm] * 8,
        out_specs=[hbm] * 5,
        out_shape=[
            jax.ShapeDtypeStruct((n_rows, width), jnp.bfloat16),
            jax.ShapeDtypeStruct((width, wide), jnp.float32),
            out, out, out,
        ],
        scratch_shapes=[
            pltpu.VMEM((n_rows, width), jnp.bfloat16),
            pltpu.VMEM((width, n_rows), jnp.bfloat16),
            pltpu.VMEM((width, 4 * wide), jnp.bfloat16),
            pltpu.VMEM((n_rows, 4 * wide), jnp.int32),
            pltpu.VMEM((n_rows, 1), jnp.float32),
            pltpu.VMEM((1, 4 * wide), jnp.float32),
            pltpu.VMEM((n_rows, 4 * wide), jnp.bfloat16),
            pltpu.VMEM((n_rows, width), jnp.bfloat16),
            pltpu.VMEM((width, wide), jnp.float32),
            pltpu.VMEM((3, width, wide), jnp.bfloat16),
            pltpu.SemaphoreType.DMA((11,)),
            pltpu.SemaphoreType.DMA((5,)),
        ],
        compiler_params=pltpu.CompilerParams(vmem_limit_bytes=VMEM_LIMIT),
        cost_estimate=pl.CostEstimate(
            flops=6 * n_rows * 4 * wide * width,
            bytes_accessed=4 * n_rows * 4 * wide,
            transcendentals=3 * n_rows * 4 * wide,
        ),
    )(place, rows, *pieces, counts, row_term, col_term)


def adagrad(emb, acc, grad):
    acc = acc + grad * grad
    return (emb - 0.1 * grad / jnp.sqrt(acc), acc)


def on_device(row_emb, row_acc, col_emb, col_acc, counts, row_marg, col_marg):
    n_row, n_col = lax.axis_size("row"), lax.axis_size("col")
    width = row_emb.shape[0]
    rows, cols = counts.shape
    half = cols // n_row
    row_scale = 1.0 / jnp.sqrt(jnp.float32(cols * n_col))
    col_scale = 1.0 / jnp.sqrt(jnp.float32(rows * n_row))
    me = lax.axis_index("row")
    odd = me % 2 == 1
    place = (me // 2).astype(jnp.int32)[None]
    row_term = (12.0 - jnp.log(row_marg.astype(jnp.float32)))[:, None]
    col_term = jnp.log(col_marg.astype(jnp.float32))[None, :]
    pair = [(i, i ^ 1) for i in range(n_row)]
    step_by = lambda d: [(i, (i // 2 + d) % 4 * 2 + i % 2) for i in range(n_row)]
    row_emb, row_acc = row_emb.T, row_acc.T
    for step in range(2):
        col_half = col_emb.astype(jnp.bfloat16)
        other = lax.ppermute(col_half, "row", pair)
        row_half = jnp.broadcast_to(row_emb.astype(jnp.bfloat16)[None], (n_col,) + row_emb.shape)
        row_half = lax.all_to_all(row_half, "col", 0, 0).reshape(rows, width)
        mine = jnp.concatenate(
            [jnp.where(odd, other, col_half), jnp.where(odd, col_half, other)], axis=1
        )
        pieces = [mine] + [lax.ppermute(mine, "row", step_by(-d)) for d in (1, 2, 3)]
        grads = tile_grads(place, row_half, pieces, counts, row_term, col_term)
        parts = lax.all_to_all(grads[0].reshape(n_col, rows // n_col, width), "col", 0, 0)
        row_grad = jnp.sum(parts.astype(jnp.float32), axis=0) * row_scale
        col_sum = grads[1]
        for d in (1, 2, 3):
            col_sum = col_sum + lax.ppermute(grads[1 + d], "row", step_by(d)).astype(jnp.float32)
        low, high = col_sum[:, :half], col_sum[:, half:]
        away = jnp.where(odd, low, high).astype(jnp.bfloat16)
        col_grad = jnp.where(odd, high, low) + lax.ppermute(away, "row", pair).astype(jnp.float32)
        row_emb, row_acc = adagrad(row_emb, row_acc, row_grad)
        col_emb, col_acc = adagrad(col_emb, col_acc, col_grad * col_scale)
    return (row_emb.T, row_acc.T, col_emb, col_acc)


def solution(mesh):
    by_row, by_col = P(None, ("row", "col")), P(None, ("col", "row"))
    return jax.shard_map(
        on_device,
        mesh=mesh,
        in_specs=(by_row, by_row, by_col, by_col, P("row", "col"), P("row"), P("col")),
        out_specs=(by_row, by_row, by_col, by_col),
        check_vma=False,
    )
```

```python
import functools

import jax
import jax.numpy as jnp
from jax import lax
from jax.experimental import pallas as pl
from jax.experimental.pallas import tpu as pltpu
from jax.sharding import PartitionSpec as P

ROW_TILE = 128
VMEM_LIMIT = 24 * 1024 * 1024
ROW_COST = 1 << 36
PAIR_COST = 1 << 36


def tile_kernel(place, rows_in, piece0, piece1, piece2, piece3, counts_in, row_term_in, col_term_in,
                rows_out, grad0, grad1, grad2, grad3,
                rows, rows_t, cols, counts, row_term, col_term, slope,
                grad_rows, grad_own, grad_away, in_sem, out_sem):
    n_rows = rows.shape[0]
    wide = piece0.shape[1]
    pieces = (piece0, piece1, piece2, piece3)
    outs = (grad0, grad1, grad2, grad3)

    def start(source, target, sem):
        copy = pltpu.make_async_copy(source, target, sem)
        copy.start()
        return copy

    def there(d):
        return pl.ds(pl.multiple_of(lax.rem(place[0] + d, 4) * wide, wide), wide)

    here = [pl.ds(d * wide, wide) for d in range(4)]
    rows_copy = start(rows_in, rows, in_sem.at[0])
    cols_copy, counts_copy = [], []
    for d in range(4):
        cols_copy.append(start(pieces[d], cols.at[:, here[d]], in_sem.at[1 + d]))
        counts_copy.append(
            start(counts_in.at[:, there(d)], counts.at[:, here[d]], in_sem.at[5 + d])
        )
        if d == 0:
            row_copy = start(row_term_in, row_term, in_sem.at[9])
            col_copy = start(col_term_in, col_term, in_sem.at[10])
    rows_copy.wait()
    rows_t[...] = rows[...].T
    done = []
    for d in range(4):
        cols_copy[d].wait()
        counts_copy[d].wait()
        if d == 0:
            row_copy.wait()
            col_copy.wait()
        col_part = col_term[:, there(d)]
        for first in range(0, n_rows, ROW_TILE):
            at = pl.ds(first, ROW_TILE)
            score = jnp.dot(rows[at, :], cols[:, here[d]], preferred_element_type=jnp.float32)
            count = counts[at, here[d]]
            value = jnp.maximum(count.astype(jnp.float32), 1.0)
            diff = score - (jnp.log(value) + (row_term[at, :] - col_part))
            weight = 0.1 + 0.25 * (value * lax.rsqrt(value))
            zero = 0.5 * jnp.tanh(0.5 * diff) + 0.5
            slope[at, here[d]] = jnp.where(count > 0, weight * diff, zero).astype(jnp.bfloat16)
        grad = jnp.dot(rows_t[...], slope[:, here[d]], preferred_element_type=jnp.float32)
        if d == 0:
            grad_own[...] = grad
            done.append(start(grad_own, outs[0], out_sem.at[0]))
        else:
            grad_away[d - 1] = grad.astype(jnp.bfloat16)
            done.append(start(grad_away.at[d - 1], outs[d], out_sem.at[d]))
    grad_rows[...] = lax.dot_general(
        slope[...], cols[...], (((1,), (1,)), ((), ())), preferred_element_type=jnp.float32
    ).astype(jnp.bfloat16)
    done.append(start(grad_rows, rows_out, out_sem.at[4]))
    for copy in done:
        copy.wait()


def tile_grads(place, rows, pieces, counts, row_term, col_term):
    n_rows, width = rows.shape
    wide = pieces[0].shape[1]
    hbm = pl.BlockSpec(memory_space=pltpu.HBM)
    out = jax.ShapeDtypeStruct((width, wide), jnp.bfloat16)
    return pl.pallas_call(
        tile_kernel,
        in_specs=[pl.BlockSpec(memory_space=pltpu.SMEM)] + [hbm] * 8,
        out_specs=[hbm] * 5,
        out_shape=[
            jax.ShapeDtypeStruct((n_rows, width), jnp.bfloat16),
            jax.ShapeDtypeStruct((width, wide), jnp.float32),
            out, out, out,
        ],
        scratch_shapes=[
            pltpu.VMEM((n_rows, width), jnp.bfloat16),
            pltpu.VMEM((width, n_rows), jnp.bfloat16),
            pltpu.VMEM((width, 4 * wide), jnp.bfloat16),
            pltpu.VMEM((n_rows, 4 * wide), jnp.int32),
            pltpu.VMEM((n_rows, 1), jnp.float32),
            pltpu.VMEM((1, 4 * wide), jnp.float32),
            pltpu.VMEM((n_rows, 4 * wide), jnp.bfloat16),
            pltpu.VMEM((n_rows, width), jnp.bfloat16),
            pltpu.VMEM((width, wide), jnp.float32),
            pltpu.VMEM((3, width, wide), jnp.bfloat16),
            pltpu.SemaphoreType.DMA((11,)),
            pltpu.SemaphoreType.DMA((5,)),
        ],
        compiler_params=pltpu.CompilerParams(vmem_limit_bytes=VMEM_LIMIT),
        cost_estimate=pl.CostEstimate(
            flops=6 * n_rows * 4 * wide * width,
            bytes_accessed=4 * n_rows * 4 * wide,
            transcendentals=3 * n_rows * 4 * wide,
        ),
    )(place, rows, *pieces, counts, row_term, col_term)


def adagrad(emb, acc, grad):
    acc = acc + grad * grad
    return (emb - 0.1 * grad / jnp.sqrt(acc), acc)


def whole_call(kernel, outs, cost, extra=None):
    specs = {} if extra is None else {"in_specs": extra}
    return pl.pallas_call(
        kernel,
        **specs,
        out_shape=outs,
        compiler_params=pltpu.CompilerParams(vmem_limit_bytes=VMEM_LIMIT),
        cost_estimate=pl.CostEstimate(flops=cost, bytes_accessed=cost, transcendentals=cost >> 4),
    )


def row_kernel(scale, parts, emb, acc, after, emb_out, acc_out, send):
    grad = jnp.sum(parts[...].astype(jnp.float32), axis=0) * scale
    new_emb, new_acc = adagrad(emb[...], acc[...], grad)
    emb_out[...] = new_emb
    acc_out[...] = new_acc
    send[...] = jnp.broadcast_to(new_emb.astype(jnp.bfloat16)[None], send.shape)


def pair_kernel(scale, col_sum, away, emb, acc, emb_out, acc_out, send):
    grad = (col_sum[...] + away[...].astype(jnp.float32)) * scale
    new_emb, new_acc = adagrad(emb[...], acc[...], grad)
    emb_out[...] = new_emb
    acc_out[...] = new_acc
    send[...] = new_emb.astype(jnp.bfloat16)


def on_device(row_emb, row_acc, col_emb, col_acc, counts, row_marg, col_marg):
    n_row, n_col = lax.axis_size("row"), lax.axis_size("col")
    width = row_emb.shape[0]
    rows, cols = counts.shape
    half = cols // n_row
    row_scale = float((cols * n_col) ** -0.5)
    col_scale = float((rows * n_row) ** -0.5)
    me = lax.axis_index("row")
    odd = me % 2 == 1
    place = (me // 2).astype(jnp.int32)[None]
    row_term = (12.0 - jnp.log(row_marg.astype(jnp.float32)))[:, None]
    col_term = jnp.log(col_marg.astype(jnp.float32))[None, :]
    pair = [(i, i ^ 1) for i in range(n_row)]
    step_by = lambda d: [(i, (i // 2 + d) % 4 * 2 + i % 2) for i in range(n_row)]
    row_emb, row_acc = row_emb.T, row_acc.T
    full = lambda like, dtype=jnp.float32: jax.ShapeDtypeStruct(like, dtype)
    to_all = full((n_col,) + row_emb.shape, jnp.bfloat16)
    both = jnp.stack([col_emb.astype(jnp.bfloat16), col_acc.astype(jnp.bfloat16)])
    row_send = jnp.broadcast_to(row_emb.astype(jnp.bfloat16)[None], to_all.shape)
    other = lax.ppermute(both, "row", pair).astype(jnp.float32)
    in_order = lambda mine, theirs: jnp.concatenate(
        [jnp.where(odd, theirs, mine), jnp.where(odd, mine, theirs)], axis=1
    )
    pair_emb = in_order(col_emb, other[0])
    pair_acc = in_order(col_acc, other[1])
    pair_send = pair_emb.astype(jnp.bfloat16)
    vmem = pl.BlockSpec(memory_space=pltpu.VMEM)
    in_hbm = lambda values: pltpu.with_memory_space_constraint(values, pltpu.HBM)
    own = lambda wide: jnp.where(odd, wide[:, half:], wide[:, :half])
    for step in range(2):
        row_half = lax.all_to_all(row_send, "col", 0, 0).reshape(rows, width)
        pieces = [pair_send] + [lax.ppermute(pair_send, "row", step_by(-d)) for d in (1, 2, 3)]
        grads = tile_grads(place, row_half, pieces, in_hbm(counts), row_term, col_term)
        parts = lax.all_to_all(grads[0].reshape(n_col, rows // n_col, width), "col", 0, 0)
        col_sum = grads[1]
        for d in (1, 2, 3):
            col_sum = col_sum + lax.ppermute(grads[1 + d], "row", step_by(d)).astype(jnp.float32)
        if step == 0:
            half_sum = col_sum.astype(jnp.bfloat16)
            away = lax.ppermute(half_sum, "row", pair)
            row_emb, row_acc, row_send = whole_call(
                functools.partial(row_kernel, row_scale),
                [full(row_emb.shape), full(row_emb.shape), to_all],
                ROW_COST,
                [vmem, vmem, vmem, pl.BlockSpec(memory_space=pl.ANY)],
            )(parts, row_emb, row_acc, half_sum)
            pair_emb, pair_acc, pair_send = whole_call(
                functools.partial(pair_kernel, col_scale),
                [full(pair_emb.shape), full(pair_emb.shape), full(pair_emb.shape, jnp.bfloat16)],
                PAIR_COST,
            )(col_sum, away, pair_emb, pair_acc)
        else:
            row_grad = jnp.sum(parts.astype(jnp.float32), axis=0) * row_scale
            row_emb, row_acc = adagrad(row_emb, row_acc, row_grad)
            away = jnp.where(odd, col_sum[:, :half], col_sum[:, half:]).astype(jnp.bfloat16)
            away = lax.ppermute(away, "row", pair).astype(jnp.float32)
            col_grad = (own(col_sum) + away) * col_scale
            col_emb, col_acc = adagrad(own(pair_emb), own(pair_acc), col_grad)
    return (row_emb.T, row_acc.T, col_emb, col_acc)


def solution(mesh):
    by_row, by_col = P(None, ("row", "col")), P(None, ("col", "row"))
    return jax.shard_map(
        on_device,
        mesh=mesh,
        in_specs=(by_row, by_row, by_col, by_col, P("row", "col"), P("row"), P("col")),
        out_specs=(by_row, by_row, by_col, by_col),
        check_vma=False,
    )
```

```python
import functools

import jax
import jax.numpy as jnp
from jax import lax
from jax.experimental import pallas as pl
from jax.experimental.pallas import tpu as pltpu
from jax.sharding import PartitionSpec as P

ROW_TILE = 128
VMEM_LIMIT = 24 * 1024 * 1024
TILE_COST = 16
ROW_COST = 1 << 36
PAIR_COST = 1 << 36


def tile_kernel(steps, first, place, rows_in, piece0, piece1, counts_in, row_term_in, col_term_in,
                *refs):
    if first:
        rows_out, grad0, grad1 = refs[:3]
    else:
        part_in, rows_out, grad0, grad1 = refs[:4]
    (rows, rows_t, cols, counts, row_term, col_term, slope, part,
     grad_rows, grad_own, grad_away, in_sem, out_sem) = refs[-13:]
    n_rows = rows.shape[0]
    wide = piece0.shape[1]
    pieces = (piece0, piece1)
    outs = (grad0, grad1)

    def start(source, target, sem):
        copy = pltpu.make_async_copy(source, target, sem)
        copy.start()
        return copy

    def there(k):
        return pl.ds(pl.multiple_of(lax.rem(place[0] + steps[k], 4) * wide, wide), wide)

    here = [pl.ds(k * wide, wide) for k in range(2)]
    rows_copy = start(rows_in, rows, in_sem.at[0])
    cols_copy, counts_copy = [], []
    for k in range(2):
        cols_copy.append(start(pieces[k], cols.at[:, here[k]], in_sem.at[1 + k]))
        counts_copy.append(
            start(counts_in.at[:, there(k)], counts.at[:, here[k]], in_sem.at[3 + k])
        )
        if k == 0:
            row_copy = start(row_term_in, row_term, in_sem.at[5])
            col_copy = start(col_term_in, col_term, in_sem.at[6])
    if not first:
        part_copy = start(part_in, part, in_sem.at[7])
    rows_copy.wait()
    rows_t[...] = rows[...].T
    done = []
    for k in range(2):
        cols_copy[k].wait()
        counts_copy[k].wait()
        if k == 0:
            row_copy.wait()
            col_copy.wait()
        col_part = col_term[:, there(k)]
        for top in range(0, n_rows, ROW_TILE):
            at = pl.ds(top, ROW_TILE)
            score = jnp.dot(rows[at, :], cols[:, here[k]], preferred_element_type=jnp.float32)
            count = counts[at, here[k]]
            value = jnp.maximum(count.astype(jnp.float32), 1.0)
            diff = score - (jnp.log(value) + (row_term[at, :] - col_part))
            weight = 0.1 + 0.25 * (value * lax.rsqrt(value))
            zero = 0.5 * jnp.tanh(0.5 * diff) + 0.5
            slope[at, here[k]] = jnp.where(count > 0, weight * diff, zero).astype(jnp.bfloat16)
        grad = jnp.dot(rows_t[...], slope[:, here[k]], preferred_element_type=jnp.float32)
        if steps[k] == 0:
            grad_own[...] = grad
            done.append(start(grad_own, outs[k], out_sem.at[k]))
        else:
            grad_away[k] = grad.astype(jnp.bfloat16)
            done.append(start(grad_away.at[k], outs[k], out_sem.at[k]))
    total = lax.dot_general(
        slope[...], cols[...], (((1,), (1,)), ((), ())), preferred_element_type=jnp.float32
    )
    if first:
        part[...] = total
        done.append(start(part, rows_out, out_sem.at[2]))
    else:
        part_copy.wait()
        grad_rows[...] = (part[...] + total).astype(jnp.bfloat16)
        done.append(start(grad_rows, rows_out, out_sem.at[2]))
    for copy in done:
        copy.wait()


def tile_grads(steps, place, rows, pieces, counts, row_term, col_term, part=None):
    first = part is None
    n_rows, width = rows.shape
    wide = pieces[0].shape[1]
    hbm = pl.BlockSpec(memory_space=pltpu.HBM)
    shape = jax.ShapeDtypeStruct
    return pl.pallas_call(
        functools.partial(tile_kernel, steps, first),
        in_specs=[pl.BlockSpec(memory_space=pltpu.SMEM)] + [hbm] * (6 if first else 7),
        out_specs=[hbm] * 3,
        out_shape=[
            shape((n_rows, width), jnp.float32 if first else jnp.bfloat16),
            shape((width, wide), jnp.float32 if steps[0] == 0 else jnp.bfloat16),
            shape((width, wide), jnp.bfloat16),
        ],
        scratch_shapes=[
            pltpu.VMEM((n_rows, width), jnp.bfloat16),
            pltpu.VMEM((width, n_rows), jnp.bfloat16),
            pltpu.VMEM((width, 2 * wide), jnp.bfloat16),
            pltpu.VMEM((n_rows, 2 * wide), jnp.int32),
            pltpu.VMEM((n_rows, 1), jnp.float32),
            pltpu.VMEM((1, 4 * wide), jnp.float32),
            pltpu.VMEM((n_rows, 2 * wide), jnp.bfloat16),
            pltpu.VMEM((n_rows, width), jnp.float32),
            pltpu.VMEM((n_rows, width), jnp.bfloat16),
            pltpu.VMEM((width, wide), jnp.float32),
            pltpu.VMEM((2, width, wide), jnp.bfloat16),
            pltpu.SemaphoreType.DMA((8,)),
            pltpu.SemaphoreType.DMA((3,)),
        ],
        compiler_params=pltpu.CompilerParams(vmem_limit_bytes=VMEM_LIMIT),
        cost_estimate=pl.CostEstimate(
            flops=6 * n_rows * 2 * wide * width * TILE_COST,
            bytes_accessed=4 * n_rows * 2 * wide,
            transcendentals=3 * n_rows * 2 * wide,
        ),
    )(place, rows, *pieces, counts, row_term, col_term, *(() if first else (part,)))


def adagrad(emb, acc, grad):
    acc = acc + grad * grad
    return (emb - 0.1 * grad / jnp.sqrt(acc), acc)


def whole_call(kernel, outs, cost, extra=None):
    specs = {} if extra is None else {"in_specs": extra}
    return pl.pallas_call(
        kernel,
        **specs,
        out_shape=outs,
        compiler_params=pltpu.CompilerParams(vmem_limit_bytes=VMEM_LIMIT),
        cost_estimate=pl.CostEstimate(flops=cost, bytes_accessed=cost, transcendentals=cost >> 4),
    )


def row_kernel(scale, near, far, emb, acc, after, emb_out, acc_out, send):
    grad = (near[...] + far[...]) * scale
    new_emb, new_acc = adagrad(emb[...], acc[...], grad)
    emb_out[...] = new_emb
    acc_out[...] = new_acc
    send[...] = jnp.broadcast_to(new_emb.astype(jnp.bfloat16)[None], send.shape)


def pair_kernel(scale, col_sum, away, emb, acc, emb_out, acc_out, send):
    grad = (col_sum[...] + away[...].astype(jnp.float32)) * scale
    new_emb, new_acc = adagrad(emb[...], acc[...], grad)
    emb_out[...] = new_emb
    acc_out[...] = new_acc
    send[...] = new_emb.astype(jnp.bfloat16)


def on_device(row_emb, row_acc, col_emb, col_acc, counts, row_marg, col_marg):
    n_row, n_col = lax.axis_size("row"), lax.axis_size("col")
    width = row_emb.shape[0]
    rows, cols = counts.shape
    half = cols // n_row
    row_scale = float((cols * n_col) ** -0.5)
    col_scale = float((rows * n_row) ** -0.5)
    me = lax.axis_index("row")
    odd = me % 2 == 1
    place = (me // 2).astype(jnp.int32)[None]
    row_term = (12.0 - jnp.log(row_marg.astype(jnp.float32)))[:, None]
    col_term = jnp.log(col_marg.astype(jnp.float32))[None, :]
    pair = [(i, i ^ 1) for i in range(n_row)]
    step_by = lambda d: [(i, (i // 2 + d) % 4 * 2 + i % 2) for i in range(n_row)]
    row_emb, row_acc = row_emb.T, row_acc.T
    n_chip = n_col // 2
    cores = [[2 * i, 2 * i + 1] for i in range(n_chip)]
    chips = [[2 * i + core for i in range(n_chip)] for core in range(2)]
    swap = [(i, i ^ 1) for i in range(n_col)]
    second = lax.axis_index("col") % 2 == 1
    full = lambda like, dtype=jnp.float32: jax.ShapeDtypeStruct(like, dtype)
    few = row_emb.shape[0]
    to_all = full((n_chip, 2 * few, width), jnp.bfloat16)
    both = jnp.stack([col_emb.astype(jnp.bfloat16), col_acc.astype(jnp.bfloat16)])
    shared = lax.all_gather(
        jnp.stack([row_emb, row_acc]), "col", axis=1, tiled=True, axis_index_groups=cores
    )
    shared_emb, shared_acc = shared[0], shared[1]
    row_send = jnp.broadcast_to(shared_emb.astype(jnp.bfloat16)[None], to_all.shape)
    other = lax.ppermute(both, "row", pair).astype(jnp.float32)
    in_order = lambda mine, theirs: jnp.concatenate(
        [jnp.where(odd, theirs, mine), jnp.where(odd, mine, theirs)], axis=1
    )
    pair_emb = in_order(col_emb, other[0])
    pair_acc = in_order(col_acc, other[1])
    pair_send = pair_emb.astype(jnp.bfloat16)
    vmem = pl.BlockSpec(memory_space=pltpu.VMEM)
    in_hbm = lambda values: pltpu.with_memory_space_constraint(values, pltpu.HBM)
    own = lambda wide: jnp.where(odd, wide[:, half:], wide[:, :half])
    for step in range(2):
        row_half = lax.all_to_all(row_send, "col", 0, 0, axis_index_groups=chips).reshape(rows, width)
        pieces = [pair_send] + [lax.ppermute(pair_send, "row", step_by(-d)) for d in (1, 2, 3)]
        operands = (in_hbm(counts), row_term, col_term)
        part, *grads_a = tile_grads((0, 3), place, row_half, (pieces[0], pieces[3]), *operands)
        grad_rows, *grads_b = tile_grads(
            (2, 1), place, row_half, (pieces[2], pieces[1]), *operands, part
        )
        grads = [grad_rows, grads_a[0], grads_b[1], grads_b[0], grads_a[1]]
        col_sum = grads[1]
        for d in (1, 2, 3):
            col_sum = col_sum + lax.ppermute(grads[1 + d], "row", step_by(d)).astype(jnp.float32)
        if step == 0:
            half_sum = col_sum.astype(jnp.bfloat16)
            away = lax.ppermute(half_sum, "row", pair)
            parts = lax.all_to_all(
                grads[0].reshape(to_all.shape), "col", 0, 0, axis_index_groups=chips
            )
            near = jnp.sum(parts.astype(jnp.float32), axis=0)
            far = lax.ppermute(near, "col", swap)
            shared_emb, shared_acc, row_send = whole_call(
                functools.partial(row_kernel, row_scale),
                [full(shared_emb.shape), full(shared_emb.shape), to_all],
                ROW_COST,
                [vmem, vmem, vmem, vmem, pl.BlockSpec(memory_space=pl.ANY)],
            )(near, far, shared_emb, shared_acc, half_sum)
            pair_emb, pair_acc, pair_send = whole_call(
                functools.partial(pair_kernel, col_scale),
                [full(pair_emb.shape), full(pair_emb.shape), full(pair_emb.shape, jnp.bfloat16)],
                PAIR_COST,
            )(col_sum, away, pair_emb, pair_acc)
        else:
            parts = lax.all_to_all(grads[0].reshape(n_col, few, width), "col", 0, 0)
            row_grad = jnp.sum(parts.astype(jnp.float32), axis=0) * row_scale
            mine = lambda both: jnp.where(second, both[few:], both[:few])
            row_emb, row_acc = adagrad(mine(shared_emb), mine(shared_acc), row_grad)
            away = jnp.where(odd, col_sum[:, :half], col_sum[:, half:]).astype(jnp.bfloat16)
            away = lax.ppermute(away, "row", pair).astype(jnp.float32)
            col_grad = (own(col_sum) + away) * col_scale
            col_emb, col_acc = adagrad(own(pair_emb), own(pair_acc), col_grad)
    return (row_emb.T, row_acc.T, col_emb, col_acc)


def solution(mesh):
    by_row, by_col = P(None, ("row", "col")), P(None, ("col", "row"))
    return jax.shard_map(
        on_device,
        mesh=mesh,
        in_specs=(by_row, by_row, by_col, by_col, P("row", "col"), P("row"), P("col")),
        out_specs=(by_row, by_row, by_col, by_col),
        check_vma=False,
    )
```

```python
import functools

import jax
import jax.numpy as jnp
from jax import lax
from jax.experimental import pallas as pl
from jax.experimental.pallas import tpu as pltpu
from jax.sharding import PartitionSpec as P

ROW_TILE = 128
VMEM_LIMIT = 24 * 1024 * 1024
TILE_COST = 16
ROW_COST = 1 << 36
PAIR_COST = 1 << 36


def tile_kernel(steps, first, place, rows_in, piece0, piece1, counts_in, row_term_in, col_term_in,
                *refs):
    if first:
        rows_out, grad0, grad1 = refs[:3]
    else:
        part_in, rows_out, grad0, grad1 = refs[:4]
    (rows, rows_t, cols, counts, row_term, col_term, slope, part,
     grad_rows, grad_own, grad_away, in_sem, out_sem) = refs[-13:]
    n_rows = rows.shape[0]
    wide = piece0.shape[1]
    pieces = (piece0, piece1)
    outs = (grad0, grad1)

    def start(source, target, sem):
        copy = pltpu.make_async_copy(source, target, sem)
        copy.start()
        return copy

    def there(k):
        return pl.ds(pl.multiple_of(lax.rem(place[0] + steps[k], 4) * wide, wide), wide)

    here = [pl.ds(k * wide, wide) for k in range(2)]
    rows_copy = start(rows_in, rows, in_sem.at[0])
    cols_copy, counts_copy = [], []
    for k in range(2):
        cols_copy.append(start(pieces[k], cols.at[:, here[k]], in_sem.at[1 + k]))
        counts_copy.append(
            start(counts_in.at[:, there(k)], counts.at[:, here[k]], in_sem.at[3 + k])
        )
        if k == 0:
            row_copy = start(row_term_in, row_term, in_sem.at[5])
            col_copy = start(col_term_in, col_term, in_sem.at[6])
    if not first:
        part_copy = start(part_in, part, in_sem.at[7])
    rows_copy.wait()
    rows_t[...] = rows[...].T
    done = []
    for k in range(2):
        cols_copy[k].wait()
        counts_copy[k].wait()
        if k == 0:
            row_copy.wait()
            col_copy.wait()
        col_part = col_term[:, there(k)]
        for top in range(0, n_rows, ROW_TILE):
            at = pl.ds(top, ROW_TILE)
            score = jnp.dot(rows[at, :], cols[:, here[k]], preferred_element_type=jnp.float32)
            count = counts[at, here[k]]
            value = jnp.maximum(count.astype(jnp.float32), 1.0)
            diff = score - (jnp.log(value) + (row_term[at, :] - col_part))
            weight = 0.1 + 0.25 * (value * lax.rsqrt(value))
            zero = 0.5 * jnp.tanh(0.5 * diff) + 0.5
            slope[at, here[k]] = jnp.where(count > 0, weight * diff, zero).astype(jnp.bfloat16)
    total = lax.dot_general(
        slope[...], cols[...], (((1,), (1,)), ((), ())), preferred_element_type=jnp.float32
    )
    if first:
        part[...] = total
        done.append(start(part, rows_out, out_sem.at[2]))
    else:
        part_copy.wait()
        grad_rows[...] = (part[...] + total).astype(jnp.bfloat16)
        done.append(start(grad_rows, rows_out, out_sem.at[2]))
    for k in range(2):
        grad = jnp.dot(rows_t[...], slope[:, here[k]], preferred_element_type=jnp.float32)
        if steps[k] == 0:
            grad_own[...] = grad
            done.append(start(grad_own, outs[k], out_sem.at[k]))
        else:
            grad_away[k] = grad.astype(jnp.bfloat16)
            done.append(start(grad_away.at[k], outs[k], out_sem.at[k]))
    for copy in done:
        copy.wait()


def tile_grads(steps, place, rows, pieces, counts, row_term, col_term, part=None):
    first = part is None
    n_rows, width = rows.shape
    wide = pieces[0].shape[1]
    hbm = pl.BlockSpec(memory_space=pltpu.HBM)
    shape = jax.ShapeDtypeStruct
    return pl.pallas_call(
        functools.partial(tile_kernel, steps, first),
        in_specs=[pl.BlockSpec(memory_space=pltpu.SMEM)] + [hbm] * (6 if first else 7),
        out_specs=[hbm] * 3,
        out_shape=[
            shape((n_rows, width), jnp.float32 if first else jnp.bfloat16),
            shape((width, wide), jnp.float32 if steps[0] == 0 else jnp.bfloat16),
            shape((width, wide), jnp.bfloat16),
        ],
        scratch_shapes=[
            pltpu.VMEM((n_rows, width), jnp.bfloat16),
            pltpu.VMEM((width, n_rows), jnp.bfloat16),
            pltpu.VMEM((width, 2 * wide), jnp.bfloat16),
            pltpu.VMEM((n_rows, 2 * wide), jnp.int32),
            pltpu.VMEM((n_rows, 1), jnp.float32),
            pltpu.VMEM((1, 4 * wide), jnp.float32),
            pltpu.VMEM((n_rows, 2 * wide), jnp.bfloat16),
            pltpu.VMEM((n_rows, width), jnp.float32),
            pltpu.VMEM((n_rows, width), jnp.bfloat16),
            pltpu.VMEM((width, wide), jnp.float32),
            pltpu.VMEM((2, width, wide), jnp.bfloat16),
            pltpu.SemaphoreType.DMA((8,)),
            pltpu.SemaphoreType.DMA((3,)),
        ],
        compiler_params=pltpu.CompilerParams(vmem_limit_bytes=VMEM_LIMIT),
        cost_estimate=pl.CostEstimate(
            flops=6 * n_rows * 2 * wide * width * TILE_COST,
            bytes_accessed=4 * n_rows * 2 * wide,
            transcendentals=3 * n_rows * 2 * wide,
        ),
    )(place, rows, *pieces, counts, row_term, col_term, *(() if first else (part,)))


def adagrad(emb, acc, grad):
    acc = acc + grad * grad
    return (emb - 0.1 * grad / jnp.sqrt(acc), acc)


def whole_call(kernel, outs, cost, extra=None):
    specs = {} if extra is None else {"in_specs": extra}
    return pl.pallas_call(
        kernel,
        **specs,
        out_shape=outs,
        compiler_params=pltpu.CompilerParams(vmem_limit_bytes=VMEM_LIMIT),
        cost_estimate=pl.CostEstimate(flops=cost, bytes_accessed=cost, transcendentals=cost >> 4),
    )


def row_kernel(scale, near, far, emb, acc, after, emb_out, acc_out, send):
    grad = (near[...] + far[...]) * scale
    new_emb, new_acc = adagrad(emb[...], acc[...], grad)
    emb_out[...] = new_emb
    acc_out[...] = new_acc
    send[...] = jnp.broadcast_to(new_emb.astype(jnp.bfloat16)[None], send.shape)


def last_kernel(scale, near, far, emb, acc, after, emb_out, acc_out):
    grad = (near[...] + far[...].astype(jnp.float32)) * scale
    new_emb, new_acc = adagrad(emb[...], acc[...], grad)
    emb_out[...] = new_emb
    acc_out[...] = new_acc


def pair_kernel(scale, col_sum, away, emb, acc, after, emb_out, acc_out, send):
    grad = (col_sum[...] + away[...].astype(jnp.float32)) * scale
    new_emb, new_acc = adagrad(emb[...], acc[...], grad)
    emb_out[...] = new_emb
    acc_out[...] = new_acc
    send[...] = new_emb.astype(jnp.bfloat16)


def on_device(row_emb, row_acc, col_emb, col_acc, counts, row_marg, col_marg):
    n_row, n_col = lax.axis_size("row"), lax.axis_size("col")
    width = row_emb.shape[0]
    rows, cols = counts.shape
    half = cols // n_row
    row_scale = float((cols * n_col) ** -0.5)
    col_scale = float((rows * n_row) ** -0.5)
    me = lax.axis_index("row")
    odd = me % 2 == 1
    place = (me // 2).astype(jnp.int32)[None]
    row_term = (12.0 - jnp.log(row_marg.astype(jnp.float32)))[:, None]
    col_term = jnp.log(col_marg.astype(jnp.float32))[None, :]
    pair = [(i, i ^ 1) for i in range(n_row)]
    step_by = lambda d: [(i, (i // 2 + d) % 4 * 2 + i % 2) for i in range(n_row)]
    row_emb, row_acc = row_emb.T, row_acc.T
    n_chip = n_col // 2
    cores = [[2 * i, 2 * i + 1] for i in range(n_chip)]
    chips = [[2 * i + core for i in range(n_chip)] for core in range(2)]
    swap = [(i, i ^ 1) for i in range(n_col)]
    second = lax.axis_index("col") % 2 == 1
    full = lambda like, dtype=jnp.float32: jax.ShapeDtypeStruct(like, dtype)
    few = row_emb.shape[0]
    to_all = full((n_chip, 2 * few, width), jnp.bfloat16)
    both = jnp.stack([col_emb.astype(jnp.bfloat16), col_acc.astype(jnp.bfloat16)])
    shared = lax.all_gather(
        jnp.stack([row_emb, row_acc]), "col", axis=1, tiled=True, axis_index_groups=cores
    )
    shared_emb, shared_acc = shared[0], shared[1]
    row_send = jnp.broadcast_to(shared_emb.astype(jnp.bfloat16)[None], to_all.shape)
    other = lax.ppermute(both, "row", pair).astype(jnp.float32)
    in_order = lambda mine, theirs: jnp.concatenate(
        [jnp.where(odd, theirs, mine), jnp.where(odd, mine, theirs)], axis=1
    )
    pair_emb = in_order(col_emb, other[0])
    pair_acc = in_order(col_acc, other[1])
    pair_send = pair_emb.astype(jnp.bfloat16)
    vmem = pl.BlockSpec(memory_space=pltpu.VMEM)
    anywhere = pl.BlockSpec(memory_space=pl.ANY)
    in_hbm = lambda values: pltpu.with_memory_space_constraint(values, pltpu.HBM)
    own = lambda wide: jnp.where(odd, wide[:, half:], wide[:, :half])
    for step in range(2):
        row_half = lax.all_to_all(row_send, "col", 0, 0, axis_index_groups=chips).reshape(rows, width)
        pieces = [pair_send] + [lax.ppermute(pair_send, "row", step_by(-d)) for d in (1, 2, 3)]
        operands = (in_hbm(counts), row_term, col_term)
        part, *grads_a = tile_grads((0, 3), place, row_half, (pieces[0], pieces[3]), *operands)
        grad_rows, *grads_b = tile_grads(
            (2, 1), place, row_half, (pieces[2], pieces[1]), *operands, part
        )
        grads = [grad_rows, grads_a[0], grads_b[1], grads_b[0], grads_a[1]]
        col_sum = grads[1]
        for d in (1, 2, 3):
            col_sum = col_sum + lax.ppermute(grads[1 + d], "row", step_by(d)).astype(jnp.float32)
        parts = lax.all_to_all(
            grads[0].reshape(to_all.shape), "col", 0, 0, axis_index_groups=chips
        )
        near = jnp.sum(parts.astype(jnp.float32), axis=0)
        if step == 0:
            far = lax.ppermute(near, "col", swap)
            half_sum = col_sum.astype(jnp.bfloat16)
            away = lax.ppermute(half_sum, "row", pair)
            shared_emb, shared_acc, row_send = whole_call(
                functools.partial(row_kernel, row_scale),
                [full(shared_emb.shape), full(shared_emb.shape), to_all],
                ROW_COST,
                [vmem, vmem, vmem, vmem, anywhere],
            )(near, far, shared_emb, shared_acc, half_sum)
            pair_emb, pair_acc, pair_send = whole_call(
                functools.partial(pair_kernel, col_scale),
                [full(pair_emb.shape), full(pair_emb.shape), full(pair_emb.shape, jnp.bfloat16)],
                PAIR_COST,
                [vmem, vmem, vmem, vmem, anywhere],
            )(col_sum, away, pair_emb, pair_acc, row_send)
        else:
            mine = lambda both: jnp.where(second, both[few:], both[:few])
            far = lax.ppermute(jnp.where(second, near[:few], near[few:]), "col", swap)
            half_sum = jnp.where(odd, col_sum[:, :half], col_sum[:, half:]).astype(jnp.bfloat16)
            away = lax.ppermute(half_sum, "row", pair)
            row_emb, row_acc = whole_call(
                functools.partial(last_kernel, row_scale),
                [full(row_emb.shape)] * 2,
                1 << 20,
                [vmem, vmem, vmem, vmem, anywhere],
            )(mine(near), far, mine(shared_emb), mine(shared_acc), half_sum)
            col_emb, col_acc = whole_call(
                functools.partial(last_kernel, col_scale),
                [full(col_emb.shape)] * 2,
                1 << 20,
                [vmem, vmem, vmem, vmem, anywhere],
            )(own(col_sum), away, own(pair_emb), own(pair_acc), row_emb)
    return (row_emb.T, row_acc.T, col_emb, col_acc)


def solution(mesh):
    by_row, by_col = P(None, ("row", "col")), P(None, ("col", "row"))
    return jax.shard_map(
        on_device,
        mesh=mesh,
        in_specs=(by_row, by_row, by_col, by_col, P("row", "col"), P("row"), P("col")),
        out_specs=(by_row, by_row, by_col, by_col),
        check_vma=False,
    )
```

```python
import functools

import jax
import jax.numpy as jnp
from jax import lax
from jax.experimental import pallas as pl
from jax.experimental.pallas import tpu as pltpu
from jax.sharding import PartitionSpec as P

ROW_TILE = 128
VMEM_LIMIT = 24 * 1024 * 1024
TILE_COST = 16
ROW_COST = 1 << 36
PAIR_COST = 1 << 36


def tile_kernel(steps, first, place, rows_in, piece0, piece1, counts_in, row_term_in, col_term_in,
                *refs):
    if first:
        rows_out, grad0, grad1 = refs[:3]
    else:
        part_in, rows_out, grad0, grad1 = refs[:4]
    (rows, rows_t, cols, counts, row_term, col_term, slope, part,
     grad_rows, grad_own, grad_away, in_sem, out_sem) = refs[-13:]
    n_rows = rows.shape[0]
    wide = piece0.shape[1]
    pieces = (piece0, piece1)
    outs = (grad0, grad1)

    def start(source, target, sem):
        copy = pltpu.make_async_copy(source, target, sem)
        copy.start()
        return copy

    def there(k):
        return pl.ds(pl.multiple_of(lax.rem(place[0] + steps[k], 4) * wide, wide), wide)

    here = [pl.ds(k * wide, wide) for k in range(2)]
    rows_copy = start(rows_in, rows, in_sem.at[0])
    cols_copy, counts_copy = [], []
    for k in range(2):
        cols_copy.append(start(pieces[k], cols.at[:, here[k]], in_sem.at[1 + k]))
        counts_copy.append(
            start(counts_in.at[:, there(k)], counts.at[:, here[k]], in_sem.at[3 + k])
        )
        if k == 0:
            row_copy = start(row_term_in, row_term, in_sem.at[5])
            col_copy = start(col_term_in, col_term, in_sem.at[6])
    if not first:
        part_copy = start(part_in, part, in_sem.at[7])
    rows_copy.wait()
    rows_t[...] = rows[...].T
    done = []
    for k in range(2):
        cols_copy[k].wait()
        counts_copy[k].wait()
        if k == 0:
            row_copy.wait()
            col_copy.wait()
        col_part = col_term[:, there(k)]
        for top in range(0, n_rows, ROW_TILE):
            at = pl.ds(top, ROW_TILE)
            score = jnp.dot(rows[at, :], cols[:, here[k]], preferred_element_type=jnp.float32)
            count = counts[at, here[k]]
            value = jnp.maximum(count.astype(jnp.float32), 1.0)
            diff = score - (jnp.log(value) + (row_term[at, :] - col_part))
            weight = 0.1 + 0.25 * (value * lax.rsqrt(value))
            zero = 0.5 * jnp.tanh(0.5 * diff) + 0.5
            slope[at, here[k]] = jnp.where(count > 0, weight * diff, zero).astype(jnp.bfloat16)
    total = lax.dot_general(
        slope[...], cols[...], (((1,), (1,)), ((), ())), preferred_element_type=jnp.float32
    )
    if first:
        part[...] = total
        done.append(start(part, rows_out, out_sem.at[2]))
    else:
        part_copy.wait()
        grad_rows[...] = (part[...] + total).astype(jnp.bfloat16)
        done.append(start(grad_rows, rows_out, out_sem.at[2]))
    for k in range(2):
        grad = jnp.dot(rows_t[...], slope[:, here[k]], preferred_element_type=jnp.float32)
        if steps[k] == 0:
            grad_own[...] = grad
            done.append(start(grad_own, outs[k], out_sem.at[k]))
        else:
            grad_away[k] = grad.astype(jnp.bfloat16)
            done.append(start(grad_away.at[k], outs[k], out_sem.at[k]))
    for copy in done:
        copy.wait()


def tile_grads(steps, place, rows, pieces, counts, row_term, col_term, part=None):
    first = part is None
    n_rows, width = rows.shape
    wide = pieces[0].shape[1]
    hbm = pl.BlockSpec(memory_space=pltpu.HBM)
    shape = jax.ShapeDtypeStruct
    return pl.pallas_call(
        functools.partial(tile_kernel, steps, first),
        in_specs=[pl.BlockSpec(memory_space=pltpu.SMEM)] + [hbm] * (6 if first else 7),
        out_specs=[hbm] * 3,
        out_shape=[
            shape((n_rows, width), jnp.float32 if first else jnp.bfloat16),
            shape((width, wide), jnp.float32 if steps[0] == 0 else jnp.bfloat16),
            shape((width, wide), jnp.bfloat16),
        ],
        scratch_shapes=[
            pltpu.VMEM((n_rows, width), jnp.bfloat16),
            pltpu.VMEM((width, n_rows), jnp.bfloat16),
            pltpu.VMEM((width, 2 * wide), jnp.bfloat16),
            pltpu.VMEM((n_rows, 2 * wide), jnp.int32),
            pltpu.VMEM((n_rows, 1), jnp.float32),
            pltpu.VMEM((1, 4 * wide), jnp.float32),
            pltpu.VMEM((n_rows, 2 * wide), jnp.bfloat16),
            pltpu.VMEM((n_rows, width), jnp.float32),
            pltpu.VMEM((n_rows, width), jnp.bfloat16),
            pltpu.VMEM((width, wide), jnp.float32),
            pltpu.VMEM((2, width, wide), jnp.bfloat16),
            pltpu.SemaphoreType.DMA((8,)),
            pltpu.SemaphoreType.DMA((3,)),
        ],
        compiler_params=pltpu.CompilerParams(vmem_limit_bytes=VMEM_LIMIT),
        cost_estimate=pl.CostEstimate(
            flops=6 * n_rows * 2 * wide * width * TILE_COST,
            bytes_accessed=4 * n_rows * 2 * wide,
            transcendentals=3 * n_rows * 2 * wide,
        ),
    )(place, rows, *pieces, counts, row_term, col_term, *(() if first else (part,)))


def adagrad(emb, acc, grad):
    acc = acc + grad * grad
    return (emb - 0.1 * grad / jnp.sqrt(acc), acc)


def whole_call(kernel, outs, cost, extra=None):
    specs = {} if extra is None else {"in_specs": extra}
    return pl.pallas_call(
        kernel,
        **specs,
        out_shape=outs,
        compiler_params=pltpu.CompilerParams(vmem_limit_bytes=VMEM_LIMIT),
        cost_estimate=pl.CostEstimate(flops=cost, bytes_accessed=cost, transcendentals=cost >> 4),
    )


def row_kernel(scale, near, far, emb, acc, after, emb_out, acc_out, send):
    grad = (near[...] + far[...]) * scale
    new_emb, new_acc = adagrad(emb[...], acc[...], grad)
    emb_out[...] = new_emb
    acc_out[...] = new_acc
    send[...] = jnp.broadcast_to(new_emb.astype(jnp.bfloat16)[None], send.shape)


def last_kernel(row_scale, col_scale, near, far, emb, acc, col_near, col_far, col_emb, col_acc,
                emb_out, acc_out, col_emb_out, col_acc_out):
    new_emb, new_acc = adagrad(emb[...], acc[...], (near[...] + far[...]) * row_scale)
    emb_out[...] = new_emb
    acc_out[...] = new_acc
    grad = (col_near[...] + col_far[...].astype(jnp.float32)) * col_scale
    new_emb, new_acc = adagrad(col_emb[...], col_acc[...], grad)
    col_emb_out[...] = new_emb
    col_acc_out[...] = new_acc


def pair_kernel(scale, col_sum, away, emb, acc, after, emb_out, acc_out, send):
    grad = (col_sum[...] + away[...].astype(jnp.float32)) * scale
    new_emb, new_acc = adagrad(emb[...], acc[...], grad)
    emb_out[...] = new_emb
    acc_out[...] = new_acc
    send[...] = new_emb.astype(jnp.bfloat16)


def on_device(row_emb, row_acc, col_emb, col_acc, counts, row_marg, col_marg):
    n_row, n_col = lax.axis_size("row"), lax.axis_size("col")
    width = row_emb.shape[0]
    rows, cols = counts.shape
    half = cols // n_row
    row_scale = float((cols * n_col) ** -0.5)
    col_scale = float((rows * n_row) ** -0.5)
    me = lax.axis_index("row")
    odd = me % 2 == 1
    place = (me // 2).astype(jnp.int32)[None]
    col_term = jnp.log(col_marg.astype(jnp.float32))[None, :]
    pair = [(i, i ^ 1) for i in range(n_row)]
    step_by = lambda d: [(i, (i // 2 + d) % 4 * 2 + i % 2) for i in range(n_row)]
    row_emb, row_acc = row_emb.T, row_acc.T
    n_chip = n_col // 2
    chips = [[2 * i + core for i in range(n_chip)] for core in range(2)]
    swap = [(i, i ^ 1) for i in range(n_col)]
    second = lax.axis_index("col") % 2 == 1
    full = lambda like, dtype=jnp.float32: jax.ShapeDtypeStruct(like, dtype)
    few = row_emb.shape[0]
    to_all = full((n_chip, 2 * few, width), jnp.bfloat16)
    both = jnp.stack([col_emb.astype(jnp.bfloat16), col_acc.astype(jnp.bfloat16)])
    row_send = jnp.broadcast_to(row_emb.astype(jnp.bfloat16)[None], (n_col, few, width))
    other = lax.ppermute(both, "row", pair).astype(jnp.float32)
    in_order = lambda mine, theirs: jnp.concatenate(
        [jnp.where(odd, theirs, mine), jnp.where(odd, mine, theirs)], axis=1
    )
    pair_emb = in_order(col_emb, other[0])
    pair_acc = in_order(col_acc, other[1])
    pair_send = pair_emb.astype(jnp.bfloat16)
    vmem = pl.BlockSpec(memory_space=pltpu.VMEM)
    anywhere = pl.BlockSpec(memory_space=pl.ANY)
    in_hbm = lambda values: pltpu.with_memory_space_constraint(values, pltpu.HBM)
    own = lambda wide: jnp.where(odd, wide[:, half:], wide[:, :half])
    for step in range(2):
        peers = chips if step else None
        row_half = lax.all_to_all(row_send, "col", 0, 0, axis_index_groups=peers).reshape(rows, width)
        pieces = [pair_send] + [lax.ppermute(pair_send, "row", step_by(-d)) for d in (1, 2, 3)]
        if step == 0:
            row_marg, pieces[3] = lax.optimization_barrier((row_marg, pieces[3]))
            row_term = (12.0 - jnp.log(row_marg.astype(jnp.float32)))[:, None]
        operands = (in_hbm(counts), row_term, col_term)
        part, *grads_a = tile_grads((0, 3), place, row_half, (pieces[0], pieces[3]), *operands)
        grad_rows, *grads_b = tile_grads(
            (2, 1), place, row_half, (pieces[2], pieces[1]), *operands, part
        )
        grads = [grad_rows, grads_a[0], grads_b[1], grads_b[0], grads_a[1]]
        col_sum = grads[1]
        for d in (1, 2, 3):
            col_sum = col_sum + lax.ppermute(grads[1 + d], "row", step_by(d)).astype(jnp.float32)
        parts = lax.all_to_all(
            grads[0].reshape(to_all.shape), "col", 0, 0, axis_index_groups=chips
        )
        near = jnp.sum(parts.astype(jnp.float32), axis=0)
        if step == 0:
            theirs = lax.ppermute(jnp.concatenate([near, row_emb, row_acc]), "col", swap)
            far = theirs[: 2 * few]
            both_cores = lambda mine, theirs: jnp.where(
                second, jnp.concatenate([theirs, mine]), jnp.concatenate([mine, theirs])
            )
            shared_emb = both_cores(row_emb, theirs[2 * few : 3 * few])
            shared_acc = both_cores(row_acc, theirs[3 * few :])
            half_sum = col_sum.astype(jnp.bfloat16)
            away = lax.ppermute(half_sum, "row", pair)
            shared_emb, shared_acc, row_send = whole_call(
                functools.partial(row_kernel, row_scale),
                [full(shared_emb.shape), full(shared_emb.shape), to_all],
                ROW_COST,
                [vmem, vmem, vmem, vmem, anywhere],
            )(near, far, shared_emb, shared_acc, half_sum)
            pair_emb, pair_acc, pair_send = whole_call(
                functools.partial(pair_kernel, col_scale),
                [full(pair_emb.shape), full(pair_emb.shape), full(pair_emb.shape, jnp.bfloat16)],
                PAIR_COST,
                [vmem, vmem, vmem, vmem, anywhere],
            )(col_sum, away, pair_emb, pair_acc, row_send)
        else:
            mine = lambda both: jnp.where(second, both[few:], both[:few])
            far = lax.ppermute(jnp.where(second, near[:few], near[few:]), "col", swap)
            half_sum = jnp.where(odd, col_sum[:, :half], col_sum[:, half:]).astype(jnp.bfloat16)
            away = lax.ppermute(half_sum, "row", pair)
            row_emb, row_acc, col_emb, col_acc = whole_call(
                functools.partial(last_kernel, row_scale, col_scale),
                [full(row_emb.shape)] * 2 + [full(col_emb.shape)] * 2,
                1 << 20,
            )(
                mine(near), far, mine(shared_emb), mine(shared_acc),
                own(col_sum), away, own(pair_emb), own(pair_acc),
            )
    return (row_emb.T, row_acc.T, col_emb, col_acc)


def solution(mesh):
    by_row, by_col = P(None, ("row", "col")), P(None, ("col", "row"))
    return jax.shard_map(
        on_device,
        mesh=mesh,
        in_specs=(by_row, by_row, by_col, by_col, P("row", "col"), P("row"), P("col")),
        out_specs=(by_row, by_row, by_col, by_col),
        check_vma=False,
    )
```
